32 devices in a mesh: groups: 2 (over y), attn: 4 (over z), expert: 2 (over x), tp: 2 (over core).
Axes of the slice: x: 2, y: 2, z: 4, core: 2. Of those that a mesh axis runs over, the one named last changes fastest.
Arguments:
- residual: bfloat16 [128, 3072], P(('groups', 'attn', 'expert', 'tp')), parts along dimension 0, may hold values from -20 to 20
- queries: bfloat16 [128, 3072], P(('groups', 'attn', 'expert', 'tp')), parts along dimension 0, may hold values from -12 to 12
- new_keys: bfloat16 [128, 512], P(('groups', 'attn', 'expert', 'tp')), parts along dimension 0, may hold values from -6 to 6
- new_values: bfloat16 [128, 512], P(('groups', 'attn', 'expert', 'tp')), parts along dimension 0, may hold values from -18 to 18
- cache_keys: bfloat16 [128, 256, 512], P(('groups', 'attn', 'expert', 'tp')), parts along dimension 0, may hold values from -6 to 6
- cache_values: bfloat16 [128, 256, 512], P(('groups', 'attn', 'expert', 'tp')), parts along dimension 0, may hold values from -18 to 18
- lengths: int32 [128], P(('groups', 'attn', 'expert', 'tp')), parts along dimension 0, may hold values from 2 to 256, as said below
- norm_gain: float32 [3072], replicated, may hold values from 0.1 to 1.9
- router: bfloat16 [3072, 8], replicated, may hold values from -0.02734375 to 0.02734375
- expert_ids: int32 [128, 4], P(('groups', 'attn', 'expert', 'tp')), parts along dimension 0, may hold values from 0 to 7, all different within a row; in each aligned block of 4 rows (0 to 3, 4 to 7, ...) at most 3 rows name the same one
- w_gate: bfloat16 [8, 3072, 5376], P('expert', None, ('attn', 'tp')), may hold values from -0.109375 to 0.109375
- w_up: bfloat16 [8, 3072, 5376], P('expert', None, ('attn', 'tp')), may hold values from -0.109375 to 0.109375
- w_down: bfloat16 [8, 5376, 3072], P('expert', ('attn', 'tp')), may hold values from -0.25 to 0.25
Outputs:
- layer_out: bfloat16 [128, 3072], P(('groups', 'attn', 'expert', 'tp')), parts along dimension 0
The draws below stay inside these ranges and needn't reach their ends.
There are 2 independent parts, one for each index of `groups`. The reference program is written for one: setup_inputs(seed, part) draws one part's arguments, and reference() takes and returns one part's arrays. A program takes and returns all parts, laid end to end along the dimension named above; an argument that names none is the same for every part. Nothing has to cross between parts.
Inputs may be any that keep to these rules, and one draw needn't show every extreme that they name: `expert_ids`: each row names 4 different experts. Within the rows of one device (aligned blocks of 4 rows) no expert is named more than 3 times, a bound that some block reaches. `lengths`: some request holds exactly 256 cached tokens.
All inputs are finite; a program needn't handle non-finite values.
Results may differ from the reference program's by a relative error of at most 0.01.
Values may be sent and summed in bfloat16 or wider, within the bound.
A program may use at most 128 MiB of HBM per device.

```python
import math
import jax
import jax.numpy as jnp
import numpy as np
from jax import lax

HEADS = 24
KV_HEADS = 4
HEAD_DIM = 128
D = 3072
FF = 5376
EXPERTS = 8
TOPK = 4
BATCH_DEV = 4
LEN = 256
CAP = 3
ROWS = 64
N_ATTN = 4
N_EXPERT = 2
N_TP = 2


def draw_queries(key, part):
    key = jax.random.fold_in(key, 3)
    full_shape = (ROWS, KV_HEADS, HEADS // KV_HEADS, HEAD_DIM)
    sample = jnp.clip(jax.random.normal(key, full_shape, jnp.float32), -6.0, 6.0)
    return sample.reshape(ROWS, HEADS * HEAD_DIM).astype(jnp.bfloat16)


def draw_cache_keys(key, part):
    key = jax.random.fold_in(key, 5)
    full_shape = (ROWS, LEN, KV_HEADS, HEAD_DIM)
    sample = jnp.clip(jax.random.normal(key, full_shape, jnp.float32), -6.0, 6.0)
    return sample.reshape(ROWS, LEN, KV_HEADS * HEAD_DIM).astype(jnp.bfloat16)


def draw_residual(key, part):
    key = jax.random.fold_in(key, 11)
    key_one, key_two, key_three = jax.random.split(key, 3)
    row_scale = jnp.exp(jax.random.uniform(key_one, (ROWS, 1), jnp.float32, 0.0, 2.302585))
    column_scale = jnp.exp(jax.random.uniform(key_two, (1, D), jnp.float32, 0.0, 2.302585))
    sample = jnp.clip(jax.random.normal(key_three, (ROWS, D), jnp.float32), -4.0, 4.0)
    return (0.05 * sample * row_scale * column_scale).astype(jnp.bfloat16)


def draw_lengths(key, part):
    key = jax.random.fold_in(key, 7)
    key_one, key_two = jax.random.split(key, 2)
    sample = jax.random.randint(key_one, (ROWS,), 2, LEN + 1)
    longest = jax.random.randint(key_two, (), 0, ROWS)
    return jnp.where(jnp.arange(ROWS) == longest, LEN, sample).astype(jnp.int32)


def block_scale(own_key, extent, pieces, smallest, top_value):
    loudness, own = 1.0, jax.random.fold_in(own_key, 6)
    for axis_at, parts in pieces:
        draws = jnp.exp(jax.random.uniform(jax.random.fold_in(own, axis_at), (parts,), jnp.float32, smallest / len(pieces), top_value / len(pieces)))
        loudness = loudness * jnp.repeat(draws, extent[axis_at] // parts).reshape([-1 if axis == axis_at else 1 for axis in range(len(extent))])
    return loudness


def deal_out(own_key, own, number, rows, amount, top, reach, lean):
    sequence = jax.random.permutation(own_key, amount)
    heavy_load, usual = shares(amount, rows * top, reach, lean, True), shares(amount, rows * top, reach, lean, False)
    places = jnp.arange(amount)

    def named(tallies, turn):
        used = int((tallies > 0).sum())
        fixed = max(1, used // 4)
        moved = fixed + (places - fixed + turn * (used - fixed)) % max(1, amount - fixed)
        return jnp.zeros((amount,), jnp.int32).at[sequence[jnp.where(places < fixed, places, moved)]].set(jnp.asarray(tallies, jnp.int32))

    tallies = jnp.where(number % 4 == 0, named(heavy_load, number // 4), named(usual, number - number // 4 - 1))
    mixed = jax.random.permutation(jax.random.fold_in(own, 3), amount)
    donor, sink = mixed[0:amount // 2 * 2:2], mixed[1:amount // 2 * 2:2]
    slack = jnp.minimum(tallies[donor] - 1, reach - tallies[sink]) // 2
    slack = jnp.where((donor == sequence[0]) | (sink == sequence[0]) | (tallies[sink] == 0), 0, jnp.maximum(slack, 0))
    moved = jax.random.randint(jax.random.fold_in(own, 4), (amount // 2,), 0, 1 << 20) % (slack + 1)
    tallies = tallies.at[donor].add(-moved).at[sink].add(moved)
    items = jnp.searchsorted(jnp.cumsum(tallies), jnp.arange(rows * top), side="right").astype(jnp.int32)
    listing = items.reshape(top, rows).T
    listing = listing[jax.random.permutation(jax.random.fold_in(own, 1), rows)]
    turn = jax.random.randint(jax.random.fold_in(own, 2), (rows, 1), 0, top)
    return jnp.take_along_axis(listing, (jnp.arange(top)[None, :] + turn) % top, axis=1)


def shares(amount, total, reach, skew, full):
    loads = [(1 << 20) // math.isqrt(rank ** skew) + 1 for rank in range(1, amount + 1)]
    largest = reach if full else min(reach, max(-(-total // amount), total * loads[0] // sum(loads)))
    least = 1 if total - largest >= amount - 1 else 0
    counts, surplus = [largest] + [least] * (amount - 1), total - largest - least * (amount - 1)
    while surplus > 0:
        movable = [i for i in range(1, amount) if counts[i] < largest] or [i for i in range(1, amount) if counts[i] < reach]
        whole, left = sum([loads[i] for i in movable]), surplus
        for i in movable:
            extra = min(reach - counts[i], max(1, left * loads[i] // whole), surplus)
            counts[i] = counts[i] + extra
            surplus = surplus - extra
    return np.array(counts)


def bell_draw(key, extent, deviation, most, pieces=(), held_as=jnp.bfloat16):
    result = deviation * jax.random.normal(key, extent, jnp.float32)
    if pieces:
        result = result * block_scale(key, extent, pieces, -0.22, 0.18)
    return jnp.clip(result, -most, most).astype(held_as)


def setup_inputs(seed: int = 0, part: int = 0) -> dict:
    arg_keys = jax.random.split(jax.random.key(seed), 14)
    own_keys = jax.random.split(jax.random.fold_in(arg_keys[13], part), 14)
    residual = draw_residual(jax.random.fold_in(jax.random.fold_in(arg_keys[13], part), 71), part)
    queries = draw_queries(jax.random.fold_in(jax.random.fold_in(arg_keys[13], part), 71), part)
    new_keys = bell_draw(own_keys[2], (ROWS, KV_HEADS * HEAD_DIM), 1.0, 6.0, ((0, 16),))
    new_values = bell_draw(own_keys[3], (ROWS, KV_HEADS * HEAD_DIM), 3.0, 18.0, ((0, 16),))
    cache_keys = draw_cache_keys(jax.random.fold_in(jax.random.fold_in(arg_keys[13], part), 71), part)
    cache_values = bell_draw(own_keys[5], (ROWS, LEN, KV_HEADS * HEAD_DIM), 3.0, 18.0, ((0, 16),))
    lengths = draw_lengths(jax.random.fold_in(jax.random.fold_in(arg_keys[13], part), 71), part)
    norm_gain = jnp.clip(1.0 + 0.18 * jax.random.normal(arg_keys[7], (D,), jnp.float32), 0.1, 1.9)
    router = bell_draw(arg_keys[8], (D, EXPERTS), (16 * D) ** -0.5, 0.02734375)
    expert_ids_keys = jax.random.split(jax.random.fold_in(own_keys[9], 1), ROWS // BATCH_DEV)
    expert_ids_turns = jax.random.permutation(jax.random.fold_in(own_keys[9], 3), ROWS // BATCH_DEV)
    expert_ids = jax.vmap(lambda own, number: deal_out(jax.random.fold_in(own_keys[9], 2), own, number, BATCH_DEV, EXPERTS, TOPK, CAP, 2))(expert_ids_keys, expert_ids_turns).reshape((ROWS, TOPK))
    w_gate = bell_draw(arg_keys[10], (EXPERTS, D, FF), D ** -0.5, 0.109375, ((0, 2), (2, 8)))
    w_up = bell_draw(arg_keys[11], (EXPERTS, D, FF), D ** -0.5, 0.109375, ((0, 2), (2, 8)))
    w_down = bell_draw(arg_keys[12], (EXPERTS, FF, D), (FF // 8) ** -0.5, 0.25, ((0, 2), (1, 8)))
    return dict(residual=residual, queries=queries, new_keys=new_keys, new_values=new_values, cache_keys=cache_keys, cache_values=cache_values, lengths=lengths, norm_gain=norm_gain, router=router, expert_ids=expert_ids, w_gate=w_gate, w_up=w_up, w_down=w_down)


norm_eps = 1e-05

def attend_cache(queries, new_keys, new_values, cache_keys, cache_values, lengths):
    row_count = queries.shape[0]
    group_size = HEADS // KV_HEADS
    score_scale = HEAD_DIM ** (-0.5)
    query_f = queries.astype(jnp.float32).reshape(row_count, KV_HEADS, group_size, HEAD_DIM)
    keys_f = cache_keys.astype(jnp.float32).reshape(row_count, LEN, KV_HEADS, HEAD_DIM)
    values_f = cache_values.astype(jnp.float32).reshape(row_count, LEN, KV_HEADS, HEAD_DIM)
    fresh_key = new_keys.astype(jnp.float32).reshape(row_count, KV_HEADS, HEAD_DIM)
    fresh_value = new_values.astype(jnp.float32).reshape(row_count, KV_HEADS, HEAD_DIM)
    scores = jnp.einsum('rkgd,rlkd->rkgl', query_f, keys_f) * score_scale
    live = jnp.arange(LEN)[None, :] < lengths[:, None]
    scores = jnp.where(live[:, None, None, :], scores, -jnp.inf)
    own_score = jnp.einsum('rkgd,rkd->rkg', query_f, fresh_key) * score_scale
    highest = jnp.maximum(lax.optimization_barrier(jnp.max(scores, axis=-1)), own_score)
    weights = jnp.exp(scores - highest[..., None])
    own_weight = jnp.exp(own_score - highest)
    denominator = lax.optimization_barrier(jnp.sum(weights, axis=-1)) + own_weight
    probabilities = (weights / denominator[..., None]).astype(jnp.bfloat16)
    own_prob = (own_weight / denominator).astype(jnp.bfloat16)
    attended = jnp.einsum('rkgl,rlkd->rkgd', probabilities.astype(jnp.float32), values_f)
    attended = attended + own_prob.astype(jnp.float32)[..., None] * fresh_value[:, :, None, :]
    return attended.reshape(row_count, HEADS * HEAD_DIM)

def normalize(residual, attended, norm_gain):
    stream = residual.astype(jnp.float32) + attended
    average = lax.optimization_barrier(jnp.mean(stream, axis=-1, keepdims=True))
    centered = stream - average
    variance = lax.optimization_barrier(jnp.mean(centered * centered, axis=-1, keepdims=True))
    normed = (centered * lax.rsqrt(variance + norm_eps) * norm_gain.astype(jnp.float32)).astype(jnp.bfloat16)
    return (stream, normed)

def reference(residual, queries, new_keys, new_values, cache_keys, cache_values, lengths, norm_gain, router, expert_ids, w_gate, w_up, w_down):
    attended = attend_cache(queries, new_keys, new_values, cache_keys, cache_values, lengths)
    stream, normed = normalize(residual, attended, norm_gain)
    logits = jnp.dot(normed, router, preferred_element_type=jnp.float32)
    chosen = jnp.take_along_axis(logits, expert_ids, axis=1)
    gates = jax.nn.softmax(chosen, axis=-1)
    slot_total = CAP * N_ATTN * N_EXPERT * N_TP
    block_count = N_ATTN * N_TP
    block_width = FF // block_count

    def one_expert(carried, inputs_xs):
        expert, gate_w, up_w, down_w = inputs_xs
        is_named = expert_ids == expert
        row_weight = lax.optimization_barrier(jnp.sum(jnp.where(is_named, gates, 0.0), axis=1))
        taken = jnp.any(is_named, axis=1)
        row_index = jnp.nonzero(taken, size=slot_total, fill_value=0)[0].astype(jnp.int32)
        valid = jnp.arange(slot_total) < jnp.sum(taken.astype(jnp.int32))
        inputs = normed[row_index]
        gate_act = jnp.dot(inputs, gate_w, preferred_element_type=jnp.float32)
        up_act = jnp.dot(inputs, up_w, preferred_element_type=jnp.float32)
        hidden = (jax.nn.silu(gate_act) * up_act).astype(jnp.bfloat16)
        hidden_blocks = hidden.reshape(slot_total, block_count, block_width).transpose(1, 0, 2)
        down_blocks = down_w.reshape(block_count, block_width, D)

        def add_block(summed, pair):
            product = jnp.dot(pair[0], pair[1], preferred_element_type=jnp.float32).astype(jnp.bfloat16)
            product = lax.optimization_barrier(product)
            return (summed + product.astype(jnp.float32), None)
        summed, _ = lax.scan(add_block, jnp.zeros((slot_total, D), jnp.float32), (hidden_blocks, down_blocks))
        expert_out = lax.optimization_barrier(summed.astype(jnp.bfloat16))
        scaled = jnp.where(valid[:, None], row_weight[row_index][:, None] * expert_out.astype(jnp.float32), 0.0)
        return (carried.at[row_index].add(scaled), None)
    experts_all = jnp.arange(EXPERTS, dtype=jnp.int32)
    layer_total, _ = lax.scan(one_expert, stream, (experts_all, w_gate, w_up, w_down))
    return layer_total.astype(jnp.bfloat16)
```

```python
import functools

import jax
import jax.numpy as jnp
from jax import lax
from jax.experimental import pallas as pl
from jax.experimental.pallas import tpu as pltpu
from jax.sharding import PartitionSpec as P

HEADS = 24
KV_HEADS = 4
HEAD_DIM = 128
EXPERTS = 8
TOPK = 4
NORM_EPS = 1e-05
MESH = pl.DeviceIdType.MESH


def kernel(
    sizes,
    residual_ref,
    queries_ref,
    new_keys_ref,
    new_values_ref,
    lengths_ref,
    gain_ref,
    router_ref,
    ids_ref,
    keys_hbm,
    values_hbm,
    gate_hbm,
    up_hbm,
    down_hbm,
    out_ref,
    keys_ref,
    values_ref,
    gate_ref,
    up_ref,
    down_ref,
    query_rows,
    stream_ref,
    gathered,
    stage,
    rows_ref,
    weights_ref,
    hidden_ref,
    part_f32,
    part_b16,
    part_in,
    half_f32,
    half_b16,
    half_in,
    quad_f32,
    quad_b16,
    quad_in,
    cache_sem,
    gate_sem,
    up_sem,
    down_sem,
    ga_send,
    ga_recv,
    gx_send,
    gx_recv,
    gc_send,
    gc_recv,
    rc_send,
    rc_recv,
    rx_send,
    rx_recv,
    ra_send,
    ra_recv,
):
    n_attn, n_expert, n_tp, chunks = sizes
    a = lax.axis_index("attn")
    e = lax.axis_index("expert")
    t = lax.axis_index("tp")
    batch, width = residual_ref.shape
    local, ff, _ = gate_hbm.shape
    cache_len = keys_hbm.shape[1]
    kv_width = keys_hbm.shape[2]
    group_size = HEADS // KV_HEADS
    chunk = width // chunks
    total_rows = rows_ref.shape[0]

    cache_copies = [
        pltpu.make_async_copy(keys_hbm, keys_ref, cache_sem.at[0]),
        pltpu.make_async_copy(values_hbm, values_ref, cache_sem.at[1]),
    ]
    for copy in cache_copies:
        copy.start()

    def gate_copy(i):
        return pltpu.make_async_copy(gate_hbm.at[i], gate_ref.at[i], gate_sem.at[i])

    def up_copy(i):
        return pltpu.make_async_copy(up_hbm.at[i], up_ref.at[i], up_sem.at[i])

    def down_copy(c):
        columns = pl.ds(c * chunk, chunk)
        return pltpu.make_async_copy(
            down_hbm.at[:, :, columns], down_ref.at[c], down_sem.at[c]
        )

    for i in range(local):
        gate_copy(i).start()
        up_copy(i).start()
    for c in range(chunks):
        down_copy(c).start()

    barrier = pltpu.get_barrier_semaphore()
    partners = 0
    for axis, size, me in (("attn", n_attn, a), ("expert", n_expert, e), ("tp", n_tp, t)):
        for step in range(1, size):
            pl.semaphore_signal(
                barrier,
                inc=1,
                device_id={axis: lax.rem(me + step, size)},
                device_id_type=MESH,
            )
            partners += 1

    query_f = queries_ref[...].astype(jnp.float32)
    for r in range(batch):
        for h in range(HEADS):
            query_rows[r, h : h + 1, :] = query_f[
                r : r + 1, h * HEAD_DIM : (h + 1) * HEAD_DIM
            ]
    head_of = lax.broadcasted_iota(jnp.int32, (HEADS, kv_width), 0) // group_size
    kv_of = lax.broadcasted_iota(jnp.int32, (HEADS, kv_width), 1) // HEAD_DIM
    own_kv = head_of == kv_of
    position = lax.broadcasted_iota(jnp.int32, (HEADS, cache_len), 1)
    new_keys = new_keys_ref[...].astype(jnp.float32)
    new_values = new_values_ref[...].astype(jnp.float32)
    score_scale = HEAD_DIM ** (-0.5)
    for copy in cache_copies:
        copy.wait()
    for r in range(batch):
        query = query_rows[r]
        blocks = jnp.where(own_kv, jnp.concatenate([query] * KV_HEADS, axis=1), 0.0)
        scores = (
            lax.dot_general(
                blocks.astype(jnp.bfloat16),
                keys_ref[r],
                (((1,), (1,)), ((), ())),
                preferred_element_type=jnp.float32,
            )
            * score_scale
        )
        scores = jnp.where(position < lengths_ref[r], scores, -jnp.inf)
        own_score = (
            jnp.sum(blocks * new_keys[r : r + 1, :], axis=1, keepdims=True) * score_scale
        )
        highest = jnp.maximum(jnp.max(scores, axis=1, keepdims=True), own_score)
        weights = jnp.exp(scores - highest)
        own_weight = jnp.exp(own_score - highest)
        denominator = jnp.sum(weights, axis=1, keepdims=True) + own_weight
        probabilities = (weights / denominator).astype(jnp.bfloat16)
        own_prob = (own_weight / denominator).astype(jnp.bfloat16).astype(jnp.float32)
        mixed = jnp.dot(probabilities, values_ref[r], preferred_element_type=jnp.float32)
        mixed = jnp.where(own_kv, mixed + own_prob * new_values[r : r + 1, :], 0.0)
        attended = mixed[:, :HEAD_DIM]
        for k in range(1, KV_HEADS):
            attended = attended + mixed[:, k * HEAD_DIM : (k + 1) * HEAD_DIM]
        for h in range(HEADS):
            stream_ref[r : r + 1, h * HEAD_DIM : (h + 1) * HEAD_DIM] = attended[h : h + 1, :]

    stream = residual_ref[...].astype(jnp.float32) + stream_ref[...]
    stream_ref[...] = stream
    average = jnp.mean(stream, axis=1, keepdims=True)
    centered = stream - average
    variance = jnp.mean(centered * centered, axis=1, keepdims=True)
    normed = (centered * lax.rsqrt(variance + NORM_EPS) * gain_ref[...]).astype(jnp.bfloat16)

    logits = lax.dot_general(
        normed, router_ref[...], (((1,), (1,)), ((), ())), preferred_element_type=jnp.float32
    )
    expert_iota = lax.broadcasted_iota(jnp.int32, (batch, EXPERTS), 1)
    ids = ids_ref[...]
    named = expert_iota == ids[:, 0:1]
    for j in range(1, TOPK):
        named = named | (expert_iota == ids[:, j : j + 1])
    top = jnp.max(jnp.where(named, logits, -jnp.inf), axis=1, keepdims=True)
    raised = jnp.where(named, jnp.exp(logits - top), 0.0)
    gates = raised / jnp.sum(raised, axis=1, keepdims=True)
    gates_high = gates.astype(jnp.bfloat16)
    gates_low = (gates - gates_high.astype(jnp.float32)).astype(jnp.bfloat16)

    mine = gathered.at[t, e, a]
    mine[:, :width] = normed
    mine[:, width:] = jnp.zeros((batch, 256), jnp.bfloat16)
    mine[:, width : width + EXPERTS] = gates_high
    mine[:, width + 128 : width + 128 + EXPERTS] = gates_low

    pl.semaphore_wait(barrier, partners)

    def attn_send(step):
        return pltpu.make_async_remote_copy(
            src_ref=gathered.at[t, e, a],
            dst_ref=gathered.at[t, e, a],
            send_sem=ga_send.at[step],
            recv_sem=ga_recv.at[step],
            device_id={"attn": lax.rem(a + step, n_attn)},
            device_id_type=MESH,
        )

    def attn_arrived(step):
        source = lax.rem(a + n_attn - step, n_attn)
        block = gathered.at[t, e, source]
        return pltpu.make_async_remote_copy(
            src_ref=block,
            dst_ref=block,
            send_sem=ga_send.at[step],
            recv_sem=ga_recv.at[step],
            device_id={"attn": source},
            device_id_type=MESH,
        )

    def expert_copy(step, back, reverse):
        source_a = lax.rem(a + n_attn - back, n_attn)
        source_e = lax.rem(e + n_expert - step, n_expert) if reverse else e
        target_e = lax.rem(e + n_expert - step, n_expert) if reverse else lax.rem(e + step, n_expert)
        block = gathered.at[t, source_e, source_a]
        return pltpu.make_async_remote_copy(
            src_ref=block,
            dst_ref=block,
            send_sem=gx_send.at[step, back],
            recv_sem=gx_recv.at[step, back],
            device_id={"expert": target_e},
            device_id_type=MESH,
        )

    def core_copy(cstep, step, back, reverse):
        source_a = lax.rem(a + n_attn - back, n_attn)
        source_e = lax.rem(e + n_expert - step, n_expert)
        other = lax.rem(t + n_tp - cstep, n_tp)
        source_t = other if reverse else t
        target = other if reverse else lax.rem(t + cstep, n_tp)
        block = gathered.at[source_t, source_e, source_a]
        return pltpu.make_async_remote_copy(
            src_ref=block,
            dst_ref=block,
            send_sem=gc_send.at[cstep, step, back],
            recv_sem=gc_recv.at[cstep, step, back],
            device_id={"tp": target},
            device_id_type=MESH,
        )

    for step in range(1, n_attn):
        attn_send(step).start()

    def forward_all(back, _):
        for step in range(1, n_expert):
            expert_copy(step, back, False).start()
        for cstep in range(1, n_tp):
            core_copy(cstep, 0, back, False).start()

    forward_all(0, None)

    def arrived_then_forward(back, carry):
        attn_arrived(back).wait_recv()
        forward_all(back, None)
        return carry

    def crossed_then_forward(back, carry):
        for step in range(1, n_expert):
            expert_copy(step, back, True).wait_recv()
            for cstep in range(1, n_tp):
                core_copy(cstep, step, back, False).start()
        return carry

    def core_arrived(back, carry):
        for step in range(n_expert):
            for cstep in range(1, n_tp):
                core_copy(cstep, step, back, True).wait_recv()
        return carry

    lax.fori_loop(1, n_attn, arrived_then_forward, 0)
    lax.fori_loop(0, n_attn, crossed_then_forward, 0)
    lax.fori_loop(0, n_attn, core_arrived, 0)

    per_stage = 16 // batch
    attn_stages = n_attn // per_stage

    def assemble(i, carry):
        at_t = i // (n_expert * attn_stages)
        at_e = lax.rem(i // attn_stages, n_expert)
        at_a = lax.rem(i, attn_stages) * per_stage
        for j in range(per_stage):
            stage[j * batch : (j + 1) * batch, :] = gathered[at_t, at_e, at_a + j].astype(
                jnp.float32
            )
        at = pl.ds(pl.multiple_of(i * 16, 16), 16)
        rows_ref[at, :] = stage[:, :width].astype(jnp.bfloat16)
        weights_ref[at, :] = stage[:, width : width + 128] + stage[:, width + 128 :]
        return carry

    lax.fori_loop(0, total_rows // 16, assemble, 0)

    block_rows = min(total_rows, 64)
    row_blocks = total_rows // block_rows
    lane = lax.broadcasted_iota(jnp.int32, (block_rows, 128), 1)

    by_last = (((1,), (1,)), ((), ()))

    def first_products(i, carry):
        gate_copy(i).wait()
        up_copy(i).wait()

        def one_block(b, inner):
            at = pl.ds(pl.multiple_of(b * block_rows, block_rows), block_rows)
            gate_act = lax.dot_general(
                rows_ref[at, :], gate_ref[i], by_last, preferred_element_type=jnp.float32
            )
            up_act = lax.dot_general(
                rows_ref[at, :], up_ref[i], by_last, preferred_element_type=jnp.float32
            )
            valid = lane < EXPERTS
            chosen = jnp.where((lane == e * local + i) & valid, weights_ref[at, :], 0.0)
            scale = jnp.sum(chosen, axis=1, keepdims=True)
            hidden = gate_act / (1.0 + jnp.exp(-gate_act)) * up_act * scale
            hidden_ref[i, at, :] = hidden.astype(jnp.bfloat16)
            return inner

        lax.fori_loop(0, row_blocks, one_block, 0)
        return carry

    lax.fori_loop(0, local, first_products, 0)

    def core_sum(c, step, reverse):
        other = lax.rem(t + n_tp - step, n_tp) if reverse else lax.rem(t + step, n_tp)
        return pltpu.make_async_remote_copy(
            src_ref=part_b16.at[c, other],
            dst_ref=part_in.at[c, step],
            send_sem=rc_send.at[c, step],
            recv_sem=rc_recv.at[c, step],
            device_id={"tp": other},
            device_id_type=MESH,
        )

    def expert_sum(c, step, reverse):
        other = lax.rem(e + n_expert - step, n_expert) if reverse else lax.rem(e + step, n_expert)
        return pltpu.make_async_remote_copy(
            src_ref=half_b16.at[c, other],
            dst_ref=half_in.at[c, step],
            send_sem=rx_send.at[c, step],
            recv_sem=rx_recv.at[c, step],
            device_id={"expert": other},
            device_id_type=MESH,
        )

    def attn_sum(c, step, reverse):
        other = lax.rem(a + n_attn - step, n_attn) if reverse else lax.rem(a + step, n_attn)
        return pltpu.make_async_remote_copy(
            src_ref=quad_b16.at[c, other],
            dst_ref=quad_in.at[c, step],
            send_sem=ra_send.at[c, step],
            recv_sem=ra_recv.at[c, step],
            device_id={"attn": other},
            device_id_type=MESH,
        )

    tp_rows = total_rows // n_tp
    expert_rows = tp_rows // n_expert
    tp_block = min(tp_rows, 32)

    def compute_chunk(c):
        down_copy(c).wait()
        for at_t in range(n_tp):

            def one_block(b, inner, at_t=at_t):
                start = pl.multiple_of(b * tp_block, tp_block)
                at = pl.ds(start, tp_block)
                from_rows = pl.ds(pl.multiple_of(at_t * tp_rows + start, tp_block), tp_block)
                total = jnp.zeros((tp_block, chunk), jnp.float32)
                for i in range(local):
                    total = total + jnp.dot(
                        hidden_ref[i, from_rows, :],
                        down_ref[c, i],
                        preferred_element_type=jnp.float32,
                    )
                part_f32[at_t, at, :] = total
                part_b16[c, at_t, at, :] = total.astype(jnp.bfloat16)
                return inner

            if tp_rows > tp_block:
                lax.fori_loop(0, tp_rows // tp_block, one_block, 0)
            else:
                one_block(0, 0)
        half_f32[c] = part_f32[t].reshape(half_f32.shape[1:])
        for step in range(1, n_tp):
            core_sum(c, step, False).start()

    def compute_chunk_whole(c):
        down_copy(c).wait()
        total = jnp.dot(hidden_ref[0], down_ref[c, 0], preferred_element_type=jnp.float32)
        for i in range(1, local):
            total = total + jnp.dot(
                hidden_ref[i], down_ref[c, i], preferred_element_type=jnp.float32
            )
        for at_t in range(n_tp):
            piece = total[at_t * tp_rows : (at_t + 1) * tp_rows, :]
            part_f32[at_t] = piece
            part_b16[c, at_t] = piece.astype(jnp.bfloat16)
        half_f32[c] = part_f32[t].reshape(half_f32.shape[1:])
        for step in range(1, n_tp):
            core_sum(c, step, False).start()

    def after_core(c):
        for step in range(1, n_tp):
            core_sum(c, step, True).wait_recv()
        for at_e in range(n_expert):
            total = half_f32[c, at_e]
            rows = slice(at_e * expert_rows, (at_e + 1) * expert_rows)
            for step in range(1, n_tp):
                total = total + part_in[c, step, rows, :].astype(jnp.float32)
            half_f32[c, at_e] = total
            half_b16[c, at_e] = total.astype(jnp.bfloat16)
        for step in range(1, n_expert):
            expert_sum(c, step, False).start()

    def after_expert(c):
        for step in range(1, n_expert):
            expert_sum(c, step, True).wait_recv()
        total = half_f32[c, e]
        for step in range(1, n_expert):
            total = total + half_in[c, step].astype(jnp.float32)
        for at_a in range(n_attn):
            piece = total[at_a * batch : (at_a + 1) * batch, :]
            quad_f32[c, at_a] = piece
            quad_b16[c, at_a] = piece.astype(jnp.bfloat16)
        for step in range(1, n_attn):
            attn_sum(c, step, False).start()

    def after_attn(c):
        for step in range(1, n_attn):
            attn_sum(c, step, True).wait_recv()
        columns = slice(c * chunk, (c + 1) * chunk)
        total = quad_f32[c, a]
        for step in range(1, n_attn):
            total = total + quad_in[c, step].astype(jnp.float32)
        out_ref[:, columns] = (stream_ref[:, columns] + total).astype(out_ref.dtype)

    compute = compute_chunk_whole if total_rows <= 64 else compute_chunk
    for tick in range(chunks + 3):
        if tick < chunks:
            compute(tick)
        if 0 <= tick - 1 < chunks:
            after_core(tick - 1)
        if 0 <= tick - 2 < chunks:
            after_expert(tick - 2)
        if 0 <= tick - 3 < chunks:
            after_attn(tick - 3)

    for step in range(1, n_attn):
        attn_send(step).wait_send()

    def sends_done(back, carry):
        for step in range(1, n_expert):
            expert_copy(step, back, False).wait_send()
        for step in range(n_expert):
            for cstep in range(1, n_tp):
                core_copy(cstep, step, back, False).wait_send()
        return carry

    lax.fori_loop(0, n_attn, sends_done, 0)
    for c in range(chunks):
        for step in range(1, n_tp):
            core_sum(c, step, False).wait_send()
        for step in range(1, n_expert):
            expert_sum(c, step, False).wait_send()
        for step in range(1, n_attn):
            attn_sum(c, step, False).wait_send()


def body(
    residual,
    queries,
    new_keys,
    new_values,
    cache_keys,
    cache_values,
    lengths,
    norm_gain,
    router,
    expert_ids,
    w_gate,
    w_up,
    w_down,
):
    n_attn = lax.axis_size("attn")
    n_expert = lax.axis_size("expert")
    n_tp = lax.axis_size("tp")
    batch, width = residual.shape
    local, _, ff = w_gate.shape
    total_rows = n_attn * n_expert * n_tp * batch
    chunks = 4
    chunk = width // chunks
    tp_rows = total_rows // n_tp
    expert_rows = tp_rows // n_expert
    vmem = pl.BlockSpec(memory_space=pltpu.VMEM)
    anywhere = pl.BlockSpec(memory_space=pl.ANY)
    dma = pltpu.SemaphoreType.DMA
    bf16, f32 = jnp.bfloat16, jnp.float32
    return pl.pallas_call(
        functools.partial(kernel, (n_attn, n_expert, n_tp, chunks)),
        out_shape=jax.ShapeDtypeStruct((batch, width), bf16),
        in_specs=[vmem] * 4
        + [pl.BlockSpec(memory_space=pltpu.SMEM)]
        + [vmem] * 3
        + [anywhere] * 5,
        out_specs=vmem,
        scratch_shapes=[
            pltpu.VMEM(cache_keys.shape, bf16),
            pltpu.VMEM(cache_values.shape, bf16),
            pltpu.VMEM((local, ff, width), bf16),
            pltpu.VMEM((local, ff, width), bf16),
            pltpu.VMEM((chunks, local, ff, chunk), bf16),
            pltpu.VMEM((batch, HEADS, HEAD_DIM), f32),
            pltpu.VMEM((batch, width), f32),
            pltpu.VMEM((n_tp, n_expert, n_attn, batch, width + 256), bf16),
            pltpu.VMEM((16, width + 256), f32),
            pltpu.VMEM((total_rows, width), bf16),
            pltpu.VMEM((total_rows, 128), f32),
            pltpu.VMEM((local, total_rows, ff), bf16),
            pltpu.VMEM((n_tp, tp_rows, chunk), f32),
            pltpu.VMEM((chunks, n_tp, tp_rows, chunk), bf16),
            pltpu.VMEM((chunks, n_tp, tp_rows, chunk), bf16),
            pltpu.VMEM((chunks, n_expert, expert_rows, chunk), f32),
            pltpu.VMEM((chunks, n_expert, expert_rows, chunk), bf16),
            pltpu.VMEM((chunks, n_expert, expert_rows, chunk), bf16),
            pltpu.VMEM((chunks, n_attn, batch, chunk), f32),
            pltpu.VMEM((chunks, n_attn, batch, chunk), bf16),
            pltpu.VMEM((chunks, n_attn, batch, chunk), bf16),
            dma((2,)),
            dma((local,)),
            dma((local,)),
            dma((chunks,)),
            dma((n_attn,)),
            dma((n_attn,)),
            dma((n_expert, n_attn)),
            dma((n_expert, n_attn)),
            dma((n_tp, n_expert, n_attn)),
            dma((n_tp, n_expert, n_attn)),
            dma((chunks, n_tp)),
            dma((chunks, n_tp)),
            dma((chunks, n_expert)),
            dma((chunks, n_expert)),
            dma((chunks, n_attn)),
            dma((chunks, n_attn)),
        ],
        compiler_params=pltpu.CompilerParams(
            collective_id=0, has_side_effects=True, vmem_limit_bytes=63 * 1024 * 1024
        ),
    )(
        residual,
        queries,
        new_keys,
        new_values,
        lengths,
        norm_gain.reshape(1, width),
        router.T,
        expert_ids,
        cache_keys,
        cache_values,
        jnp.swapaxes(w_gate, 1, 2),
        jnp.swapaxes(w_up, 1, 2),
        w_down,
    )


def solution(mesh):
    rows = ("groups", "attn", "expert", "tp")
    return jax.shard_map(
        body,
        mesh=mesh,
        in_specs=(
            P(rows, None),
            P(rows, None),
            P(rows, None),
            P(rows, None),
            P(rows, None, None),
            P(rows, None, None),
            P(rows),
            P(),
            P(),
            P(rows, None),
            P("expert", None, ("attn", "tp")),
            P("expert", None, ("attn", "tp")),
            P("expert", ("attn", "tp"), None),
        ),
        out_specs=P(rows, None),
        check_vma=False,
    )
```

```python
import functools

import jax
import jax.numpy as jnp
from jax import lax
from jax.experimental import pallas as pl
from jax.experimental.pallas import tpu as pltpu
from jax.sharding import PartitionSpec as P

HEADS = 24
KV_HEADS = 4
HEAD_DIM = 128
EXPERTS = 8
TOPK = 4
NORM_EPS = 1e-05
MESH = pl.DeviceIdType.MESH
PACE = (3, 1, 2, 2, 1)


def kernel(
    sizes,
    residual_ref,
    queries_ref,
    new_keys_ref,
    new_values_ref,
    lengths_ref,
    gain_ref,
    router_ref,
    ids_ref,
    keys_hbm,
    values_hbm,
    gate_hbm,
    up_hbm,
    down_hbm,
    out_ref,
    keys_ref,
    values_ref,
    gate_ref,
    up_ref,
    down_ref,
    query_rows,
    stream_ref,
    gathered,
    stage,
    rows_ref,
    weights_ref,
    hidden_ref,
    part_f32,
    part_b16,
    part_in,
    quad_f32,
    quad_b16,
    quad_in,
    cache_sem,
    gate_sem,
    up_sem,
    down_sem,
    ga_send,
    ga_recv,
    gx_send,
    gx_recv,
    gc_send,
    gc_recv,
    rc_send,
    rc_recv,
    ra_send,
    ra_recv,
):
    n_attn, n_expert, n_tp, chunks = sizes
    a = lax.axis_index("attn")
    e = lax.axis_index("expert")
    t = lax.axis_index("tp")
    batch, width = residual_ref.shape
    local, ff, _ = gate_hbm.shape
    cache_len = keys_hbm.shape[1]
    kv_width = keys_hbm.shape[2]
    group_size = HEADS // KV_HEADS
    chunk = width // chunks
    total_rows = rows_ref.shape[0]
    chips = n_expert * n_attn
    chip = e * n_attn + a

    cache_copies = [
        pltpu.make_async_copy(keys_hbm, keys_ref, cache_sem.at[0]),
        pltpu.make_async_copy(values_hbm, values_ref, cache_sem.at[1]),
    ]
    for copy in cache_copies:
        copy.start()

    pieces = gate_sem.shape[1]
    piece = ff // pieces

    def gate_copy(i, p):
        rows = pl.ds(p * piece, piece)
        return pltpu.make_async_copy(
            gate_hbm.at[i, rows], gate_ref.at[i, rows], gate_sem.at[i, p]
        )

    def up_copy(i, p):
        rows = pl.ds(p * piece, piece)
        return pltpu.make_async_copy(up_hbm.at[i, rows], up_ref.at[i, rows], up_sem.at[i, p])

    def down_copy(c, i):
        columns = pl.ds(c * chunk, chunk)
        return pltpu.make_async_copy(
            down_hbm.at[i, :, columns], down_ref.at[c, i], down_sem.at[c, i]
        )

    waiting = []
    for i in range(local):
        for p in range(pieces):
            waiting.append(gate_copy(i, p))
            waiting.append(up_copy(i, p))
    for c in range(chunks):
        for i in range(local):
            waiting.append(down_copy(c, i))

    def start_weights(count):
        for _ in range(min(count, len(waiting))):
            waiting.pop(0).start()

    start_weights(PACE[0])

    barrier = pltpu.get_barrier_semaphore()
    partners = 0
    for step in range(1, chips):
        other = lax.rem(chip + step, chips)
        pl.semaphore_signal(
            barrier,
            inc=1,
            device_id={"expert": other // n_attn, "attn": lax.rem(other, n_attn)},
            device_id_type=MESH,
        )
        partners += 1
    for step in range(1, n_tp):
        pl.semaphore_signal(
            barrier, inc=1, device_id={"tp": lax.rem(t + step, n_tp)}, device_id_type=MESH
        )
        partners += 1

    query_f = queries_ref[...].astype(jnp.float32)
    for r in range(batch):
        for h in range(HEADS):
            query_rows[r, h : h + 1, :] = query_f[
                r : r + 1, h * HEAD_DIM : (h + 1) * HEAD_DIM
            ]
    head_of = lax.broadcasted_iota(jnp.int32, (HEADS, kv_width), 0) // group_size
    kv_of = lax.broadcasted_iota(jnp.int32, (HEADS, kv_width), 1) // HEAD_DIM
    own_kv = head_of == kv_of
    position = lax.broadcasted_iota(jnp.int32, (HEADS, cache_len), 1)
    new_keys = new_keys_ref[...].astype(jnp.float32)
    new_values = new_values_ref[...].astype(jnp.float32)
    score_scale = HEAD_DIM ** (-0.5)
    for copy in cache_copies:
        copy.wait()
    for r in range(batch):
        query = query_rows[r]
        blocks = jnp.where(own_kv, jnp.concatenate([query] * KV_HEADS, axis=1), 0.0)
        scores = (
            lax.dot_general(
                blocks.astype(jnp.bfloat16),
                keys_ref[r],
                (((1,), (1,)), ((), ())),
                preferred_element_type=jnp.float32,
            )
            * score_scale
        )
        scores = jnp.where(position < lengths_ref[r], scores, -jnp.inf)
        own_score = (
            jnp.sum(blocks * new_keys[r : r + 1, :], axis=1, keepdims=True) * score_scale
        )
        highest = jnp.maximum(jnp.max(scores, axis=1, keepdims=True), own_score)
        weights = jnp.exp(scores - highest)
        own_weight = jnp.exp(own_score - highest)
        denominator = jnp.sum(weights, axis=1, keepdims=True) + own_weight
        probabilities = (weights / denominator).astype(jnp.bfloat16)
        own_prob = (own_weight / denominator).astype(jnp.bfloat16).astype(jnp.float32)
        mixed = jnp.dot(probabilities, values_ref[r], preferred_element_type=jnp.float32)
        mixed = jnp.where(own_kv, mixed + own_prob * new_values[r : r + 1, :], 0.0)
        attended = mixed[:, :HEAD_DIM]
        for k in range(1, KV_HEADS):
            attended = attended + mixed[:, k * HEAD_DIM : (k + 1) * HEAD_DIM]
        for h in range(HEADS):
            stream_ref[r : r + 1, h * HEAD_DIM : (h + 1) * HEAD_DIM] = attended[h : h + 1, :]
        start_weights(PACE[1])

    stream = residual_ref[...].astype(jnp.float32) + stream_ref[...]
    stream_ref[...] = stream
    average = jnp.mean(stream, axis=1, keepdims=True)
    centered = stream - average
    variance = jnp.mean(centered * centered, axis=1, keepdims=True)
    normed = (centered * lax.rsqrt(variance + NORM_EPS) * gain_ref[...]).astype(jnp.bfloat16)

    logits = lax.dot_general(
        normed, router_ref[...], (((1,), (1,)), ((), ())), preferred_element_type=jnp.float32
    )
    expert_iota = lax.broadcasted_iota(jnp.int32, (batch, EXPERTS), 1)
    ids = ids_ref[...]
    named = expert_iota == ids[:, 0:1]
    for j in range(1, TOPK):
        named = named | (expert_iota == ids[:, j : j + 1])
    top = jnp.max(jnp.where(named, logits, -jnp.inf), axis=1, keepdims=True)
    raised = jnp.where(named, jnp.exp(logits - top), 0.0)
    gates = raised / jnp.sum(raised, axis=1, keepdims=True)
    gates_high = gates.astype(jnp.bfloat16)
    gates_low = (gates - gates_high.astype(jnp.float32)).astype(jnp.bfloat16)

    mine = gathered.at[t, e, a]
    mine[:, :width] = normed
    mine[:, width:] = jnp.zeros((batch, 256), jnp.bfloat16)
    mine[:, width : width + EXPERTS] = gates_high
    mine[:, width + 128 : width + 128 + EXPERTS] = gates_low

    pl.semaphore_wait(barrier, partners)

    def attn_send(step):
        return pltpu.make_async_remote_copy(
            src_ref=gathered.at[t, e, a],
            dst_ref=gathered.at[t, e, a],
            send_sem=ga_send.at[step],
            recv_sem=ga_recv.at[step],
            device_id={"attn": lax.rem(a + step, n_attn)},
            device_id_type=MESH,
        )

    def attn_arrived(step):
        source = lax.rem(a + n_attn - step, n_attn)
        block = gathered.at[t, e, source]
        return pltpu.make_async_remote_copy(
            src_ref=block,
            dst_ref=block,
            send_sem=ga_send.at[step],
            recv_sem=ga_recv.at[step],
            device_id={"attn": source},
            device_id_type=MESH,
        )

    def expert_copy(step, back, reverse):
        source_a = lax.rem(a + n_attn - back, n_attn)
        source_e = lax.rem(e + n_expert - step, n_expert) if reverse else e
        target_e = lax.rem(e + n_expert - step, n_expert) if reverse else lax.rem(e + step, n_expert)
        block = gathered.at[t, source_e, source_a]
        return pltpu.make_async_remote_copy(
            src_ref=block,
            dst_ref=block,
            send_sem=gx_send.at[step, back],
            recv_sem=gx_recv.at[step, back],
            device_id={"expert": target_e},
            device_id_type=MESH,
        )

    def core_copy(cstep, step, back, reverse):
        source_a = lax.rem(a + n_attn - back, n_attn)
        source_e = lax.rem(e + n_expert - step, n_expert)
        other = lax.rem(t + n_tp - cstep, n_tp)
        source_t = other if reverse else t
        target = other if reverse else lax.rem(t + cstep, n_tp)
        block = gathered.at[source_t, source_e, source_a]
        return pltpu.make_async_remote_copy(
            src_ref=block,
            dst_ref=block,
            send_sem=gc_send.at[cstep, step, back],
            recv_sem=gc_recv.at[cstep, step, back],
            device_id={"tp": target},
            device_id_type=MESH,
        )

    for step in range(1, n_attn):
        attn_send(step).start()

    def forward_all(back, _):
        for step in range(1, n_expert):
            expert_copy(step, back, False).start()
        for cstep in range(1, n_tp):
            core_copy(cstep, 0, back, False).start()

    forward_all(0, None)
    start_weights(PACE[2])

    def arrived_then_forward(back, carry):
        attn_arrived(back).wait_recv()
        forward_all(back, None)
        return carry

    def crossed_then_forward(back, carry):
        for step in range(1, n_expert):
            expert_copy(step, back, True).wait_recv()
            for cstep in range(1, n_tp):
                core_copy(cstep, step, back, False).start()
        return carry

    def core_arrived(back, carry):
        for step in range(n_expert):
            for cstep in range(1, n_tp):
                core_copy(cstep, step, back, True).wait_recv()
        return carry

    for back in range(1, n_attn):
        arrived_then_forward(back, 0)
        start_weights(PACE[3])
    for back in range(n_attn):
        crossed_then_forward(back, 0)
        start_weights(PACE[4])
    start_weights(len(waiting))
    lax.fori_loop(0, n_attn, core_arrived, 0)

    per_stage = 16 // batch
    attn_stages = n_attn // per_stage

    def assemble(i, carry):
        at_t = i // (n_expert * attn_stages)
        at_e = lax.rem(i // attn_stages, n_expert)
        at_a = lax.rem(i, attn_stages) * per_stage
        for j in range(per_stage):
            stage[j * batch : (j + 1) * batch, :] = gathered[at_t, at_e, at_a + j].astype(
                jnp.float32
            )
        at = pl.ds(pl.multiple_of(i * 16, 16), 16)
        rows_ref[at, :] = stage[:, :width].astype(jnp.bfloat16)
        weights_ref[at, :] = stage[:, width : width + 128] + stage[:, width + 128 :]
        return carry

    lax.fori_loop(0, total_rows // 16, assemble, 0)

    block_rows = min(total_rows, 64)
    row_blocks = total_rows // block_rows
    lane = lax.broadcasted_iota(jnp.int32, (block_rows, 128), 1)

    by_last = (((1,), (1,)), ((), ()))

    def first_products(i, carry):
        for p in range(pieces):
            gate_copy(i, p).wait()
            up_copy(i, p).wait()

        def one_block(b, inner):
            at = pl.ds(pl.multiple_of(b * block_rows, block_rows), block_rows)
            gate_act = lax.dot_general(
                rows_ref[at, :], gate_ref[i], by_last, preferred_element_type=jnp.float32
            )
            up_act = lax.dot_general(
                rows_ref[at, :], up_ref[i], by_last, preferred_element_type=jnp.float32
            )
            valid = lane < EXPERTS
            chosen = jnp.where((lane == e * local + i) & valid, weights_ref[at, :], 0.0)
            scale = jnp.sum(chosen, axis=1, keepdims=True)
            hidden = gate_act / (1.0 + jnp.exp(-gate_act)) * up_act * scale
            hidden_ref[i, at, :] = hidden.astype(jnp.bfloat16)
            return inner

        lax.fori_loop(0, row_blocks, one_block, 0)
        return carry

    lax.fori_loop(0, local, first_products, 0)

    def core_sum(c, step, reverse):
        other = lax.rem(t + n_tp - step, n_tp) if reverse else lax.rem(t + step, n_tp)
        return pltpu.make_async_remote_copy(
            src_ref=part_b16.at[c, other],
            dst_ref=part_in.at[c, step],
            send_sem=rc_send.at[c, step],
            recv_sem=rc_recv.at[c, step],
            device_id={"tp": other},
            device_id_type=MESH,
        )

    def chip_sum(c, step, reverse):
        other = lax.rem(chip + chips - step, chips) if reverse else lax.rem(chip + step, chips)
        return pltpu.make_async_remote_copy(
            src_ref=quad_b16.at[c, other],
            dst_ref=quad_in.at[c, step],
            send_sem=ra_send.at[c, step],
            recv_sem=ra_recv.at[c, step],
            device_id={"expert": other // n_attn, "attn": lax.rem(other, n_attn)},
            device_id_type=MESH,
        )

    tp_rows = total_rows // n_tp
    tp_block = min(tp_rows, 32)

    def compute_chunk(c):
        for i in range(local):
            down_copy(c, i).wait()
        for at_t in range(n_tp):

            def one_block(b, inner, at_t=at_t):
                start = pl.multiple_of(b * tp_block, tp_block)
                at = pl.ds(start, tp_block)
                from_rows = pl.ds(pl.multiple_of(at_t * tp_rows + start, tp_block), tp_block)
                total = jnp.zeros((tp_block, chunk), jnp.float32)
                for i in range(local):
                    total = total + jnp.dot(
                        hidden_ref[i, from_rows, :],
                        down_ref[c, i],
                        preferred_element_type=jnp.float32,
                    )
                part_f32[c, at_t, at, :] = total
                part_b16[c, at_t, at, :] = total.astype(jnp.bfloat16)
                return inner

            lax.fori_loop(0, tp_rows // tp_block, one_block, 0)
        for step in range(1, n_tp):
            core_sum(c, step, False).start()

    def compute_chunk_whole(c):
        for i in range(local):
            down_copy(c, i).wait()
        total = jnp.dot(hidden_ref[0], down_ref[c, 0], preferred_element_type=jnp.float32)
        for i in range(1, local):
            total = total + jnp.dot(
                hidden_ref[i], down_ref[c, i], preferred_element_type=jnp.float32
            )
        for at_t in range(n_tp):
            rows = total[at_t * tp_rows : (at_t + 1) * tp_rows, :]
            part_f32[c, at_t] = rows
            part_b16[c, at_t] = rows.astype(jnp.bfloat16)
        for step in range(1, n_tp):
            core_sum(c, step, False).start()

    def send_chunk(c):
        for step in range(1, n_tp):
            core_sum(c, step, True).wait_recv()

        def one_block(b, carry):
            at = pl.ds(pl.multiple_of(b * 16, 16), 16)
            total = part_f32[c, t, at, :]
            for step in range(1, n_tp):
                total = total + part_in[c, step, at, :].astype(jnp.float32)
            for j in range(per_stage):
                rows = total[j * batch : (j + 1) * batch, :]
                quad_f32[c, b * per_stage + j] = rows
                quad_b16[c, b * per_stage + j] = rows.astype(jnp.bfloat16)
            return carry

        lax.fori_loop(0, tp_rows // 16, one_block, 0)

        def one_send(step, carry):
            chip_sum(c, step, False).start()
            return carry

        lax.fori_loop(1, chips, one_send, 0)

    def finish_chunk(c):
        columns = slice(c * chunk, (c + 1) * chunk)

        def one_arrival(step, total):
            chip_sum(c, step, True).wait_recv()
            return total + quad_in[c, step].astype(jnp.float32)

        total = lax.fori_loop(1, chips, one_arrival, stream_ref[:, columns] + quad_f32[c, chip])
        out_ref[:, columns] = total.astype(out_ref.dtype)

    compute = compute_chunk_whole if total_rows <= 64 else compute_chunk
    for c in range(chunks):
        compute(c)
        if c > 0:
            send_chunk(c - 1)
    send_chunk(chunks - 1)
    for c in range(chunks):
        finish_chunk(c)

    for step in range(1, n_attn):
        attn_send(step).wait_send()

    def sends_done(back, carry):
        for step in range(1, n_expert):
            expert_copy(step, back, False).wait_send()
        for step in range(n_expert):
            for cstep in range(1, n_tp):
                core_copy(cstep, step, back, False).wait_send()
        return carry

    lax.fori_loop(0, n_attn, sends_done, 0)
    for c in range(chunks):
        for step in range(1, n_tp):
            core_sum(c, step, False).wait_send()

        def one_left(step, carry, c=c):
            chip_sum(c, step, False).wait_send()
            return carry

        lax.fori_loop(1, chips, one_left, 0)


def body(
    residual,
    queries,
    new_keys,
    new_values,
    cache_keys,
    cache_values,
    lengths,
    norm_gain,
    router,
    expert_ids,
    w_gate,
    w_up,
    w_down,
):
    n_attn = lax.axis_size("attn")
    n_expert = lax.axis_size("expert")
    n_tp = lax.axis_size("tp")
    batch, width = residual.shape
    local, _, ff = w_gate.shape
    total_rows = n_attn * n_expert * n_tp * batch
    chunks = 2
    chunk = width // chunks
    tp_rows = total_rows // n_tp
    chips = n_expert * n_attn
    pieces = 2 if ff % 32 == 0 else 1
    vmem = pl.BlockSpec(memory_space=pltpu.VMEM)
    anywhere = pl.BlockSpec(memory_space=pl.ANY)
    dma = pltpu.SemaphoreType.DMA
    bf16, f32 = jnp.bfloat16, jnp.float32
    return pl.pallas_call(
        functools.partial(kernel, (n_attn, n_expert, n_tp, chunks)),
        out_shape=jax.ShapeDtypeStruct((batch, width), bf16),
        in_specs=[vmem] * 4
        + [pl.BlockSpec(memory_space=pltpu.SMEM)]
        + [vmem] * 3
        + [anywhere] * 5,
        out_specs=vmem,
        scratch_shapes=[
            pltpu.VMEM(cache_keys.shape, bf16),
            pltpu.VMEM(cache_values.shape, bf16),
            pltpu.VMEM((local, ff, width), bf16),
            pltpu.VMEM((local, ff, width), bf16),
            pltpu.VMEM((chunks, local, ff, chunk), bf16),
            pltpu.VMEM((batch, HEADS, HEAD_DIM), f32),
            pltpu.VMEM((batch, width), f32),
            pltpu.VMEM((n_tp, n_expert, n_attn, batch, width + 256), bf16),
            pltpu.VMEM((16, width + 256), f32),
            pltpu.VMEM((total_rows, width), bf16),
            pltpu.VMEM((total_rows, 128), f32),
            pltpu.VMEM((local, total_rows, ff), bf16),
            pltpu.VMEM((chunks, n_tp, tp_rows, chunk), f32),
            pltpu.VMEM((chunks, n_tp, tp_rows, chunk), bf16),
            pltpu.VMEM((chunks, n_tp, tp_rows, chunk), bf16),
            pltpu.VMEM((chunks, chips, batch, chunk), f32),
            pltpu.VMEM((chunks, chips, batch, chunk), bf16),
            pltpu.VMEM((chunks, chips, batch, chunk), bf16),
            dma((2,)),
            dma((local, pieces)),
            dma((local, pieces)),
            dma((chunks, local)),
            dma((n_attn,)),
            dma((n_attn,)),
            dma((n_expert, n_attn)),
            dma((n_expert, n_attn)),
            dma((n_tp, n_expert, n_attn)),
            dma((n_tp, n_expert, n_attn)),
            dma((chunks, n_tp)),
            dma((chunks, n_tp)),
            dma((chunks, chips)),
            dma((chunks, chips)),
        ],
        compiler_params=pltpu.CompilerParams(
            collective_id=0, has_side_effects=True, vmem_limit_bytes=63 * 1024 * 1024
        ),
    )(
        residual,
        queries,
        new_keys,
        new_values,
        lengths,
        norm_gain.reshape(1, width),
        router.T,
        expert_ids,
        cache_keys,
        cache_values,
        jnp.swapaxes(w_gate, 1, 2),
        jnp.swapaxes(w_up, 1, 2),
        w_down,
    )


def solution(mesh):
    rows = ("groups", "attn", "expert", "tp")
    return jax.shard_map(
        body,
        mesh=mesh,
        in_specs=(
            P(rows, None),
            P(rows, None),
            P(rows, None),
            P(rows, None),
            P(rows, None, None),
            P(rows, None, None),
            P(rows),
            P(),
            P(),
            P(rows, None),
            P("expert", None, ("attn", "tp")),
            P("expert", None, ("attn", "tp")),
            P("expert", ("attn", "tp"), None),
        ),
        out_specs=P(rows, None),
        check_vma=False,
    )
```

```python
import functools

import jax
import jax.numpy as jnp
from jax import lax
from jax.experimental import pallas as pl
from jax.experimental.pallas import tpu as pltpu
from jax.sharding import PartitionSpec as P

HEADS = 24
KV_HEADS = 4
HEAD_DIM = 128
EXPERTS = 8
TOPK = 4
NORM_EPS = 1e-05
MESH = pl.DeviceIdType.MESH
PACE = (3, 1, 1, 3, 2)


def kernel(
    sizes,
    residual_ref,
    queries_ref,
    new_keys_ref,
    new_values_ref,
    lengths_ref,
    gain_ref,
    router_ref,
    ids_ref,
    keys_hbm,
    values_hbm,
    gate_hbm,
    up_hbm,
    down_hbm,
    out_ref,
    keys_ref,
    values_ref,
    gate_ref,
    up_ref,
    down_ref,
    query_rows,
    stream_ref,
    gathered,
    stage,
    rows_ref,
    weights_ref,
    hidden_ref,
    part_f32,
    part_b16,
    part_in,
    quad_f32,
    quad_b16,
    quad_in,
    cache_sem,
    gate_sem,
    up_sem,
    down_sem,
    ga_send,
    ga_recv,
    gx_send,
    gx_recv,
    gc_send,
    gc_recv,
    rc_send,
    rc_recv,
    ra_send,
    ra_recv,
):
    n_attn, n_expert, n_tp, chunks = sizes
    a = lax.axis_index("attn")
    e = lax.axis_index("expert")
    t = lax.axis_index("tp")
    batch, width = residual_ref.shape
    local, ff, _ = gate_hbm.shape
    cache_len = keys_hbm.shape[1]
    kv_width = keys_hbm.shape[2]
    group_size = HEADS // KV_HEADS
    chunk = width // chunks
    total_rows = rows_ref.shape[0]
    chips = n_expert * n_attn
    chip = e * n_attn + a

    cache_copies = [
        pltpu.make_async_copy(keys_hbm, keys_ref, cache_sem.at[0]),
        pltpu.make_async_copy(values_hbm, values_ref, cache_sem.at[1]),
    ]
    for copy in cache_copies:
        copy.start()

    pieces = gate_sem.shape[1]
    piece = ff // pieces

    def gate_copy(i, p):
        rows = pl.ds(p * piece, piece)
        return pltpu.make_async_copy(
            gate_hbm.at[i, rows], gate_ref.at[i, rows], gate_sem.at[i, p]
        )

    def up_copy(i, p):
        rows = pl.ds(p * piece, piece)
        return pltpu.make_async_copy(up_hbm.at[i, rows], up_ref.at[i, rows], up_sem.at[i, p])

    def down_copy(c, i):
        columns = pl.ds(c * chunk, chunk)
        return pltpu.make_async_copy(
            down_hbm.at[i, :, columns], down_ref.at[c, i], down_sem.at[c, i]
        )

    waiting = []
    for i in range(local):
        for p in range(pieces):
            waiting.append(gate_copy(i, p))
            waiting.append(up_copy(i, p))
    for c in range(chunks):
        for i in range(local):
            waiting.append(down_copy(c, i))

    def start_weights(count):
        for _ in range(min(count, len(waiting))):
            waiting.pop(0).start()

    start_weights(PACE[0])

    barrier = pltpu.get_barrier_semaphore()
    partners = 0
    for step in range(1, chips):
        other = lax.rem(chip + step, chips)
        pl.semaphore_signal(
            barrier,
            inc=1,
            device_id={"expert": other // n_attn, "attn": lax.rem(other, n_attn)},
            device_id_type=MESH,
        )
        partners += 1
    for step in range(1, n_tp):
        pl.semaphore_signal(
            barrier, inc=1, device_id={"tp": lax.rem(t + step, n_tp)}, device_id_type=MESH
        )
        partners += 1

    query_f = queries_ref[...].astype(jnp.float32)
    for r in range(batch):
        for h in range(HEADS):
            query_rows[r, h : h + 1, :] = query_f[
                r : r + 1, h * HEAD_DIM : (h + 1) * HEAD_DIM
            ]
    head_of = lax.broadcasted_iota(jnp.int32, (HEADS, kv_width), 0) // group_size
    kv_of = lax.broadcasted_iota(jnp.int32, (HEADS, kv_width), 1) // HEAD_DIM
    own_kv = head_of == kv_of
    position = lax.broadcasted_iota(jnp.int32, (HEADS, cache_len), 1)
    new_keys = new_keys_ref[...].astype(jnp.float32)
    new_values = new_values_ref[...].astype(jnp.float32)
    score_scale = HEAD_DIM ** (-0.5)
    blocks = [
        jnp.where(own_kv, jnp.concatenate([query_rows[r]] * KV_HEADS, axis=1), 0.0)
        for r in range(batch)
    ]
    own_score = jnp.concatenate(
        [
            jnp.sum(blocks[r] * new_keys[r : r + 1, :], axis=1, keepdims=True)
            for r in range(batch)
        ],
        axis=0,
    )
    own_score = own_score * score_scale
    cache_copies[0].wait()
    scores = []
    for r in range(batch):
        product = lax.dot_general(
            blocks[r].astype(jnp.bfloat16),
            keys_ref[r],
            (((1,), (1,)), ((), ())),
            preferred_element_type=jnp.float32,
        )
        scores.append(jnp.where(position < lengths_ref[r], product * score_scale, -jnp.inf))
    scores = jnp.concatenate(scores, axis=0)
    start_weights(PACE[1])
    highest = jnp.maximum(jnp.max(scores, axis=1, keepdims=True), own_score)
    weights = jnp.exp(scores - highest)
    own_weight = jnp.exp(own_score - highest)
    denominator = jnp.sum(weights, axis=1, keepdims=True) + own_weight
    probabilities = (weights / denominator).astype(jnp.bfloat16)
    own_prob = (own_weight / denominator).astype(jnp.bfloat16).astype(jnp.float32)
    cache_copies[1].wait()
    for r in range(batch):
        of_request = slice(r * HEADS, (r + 1) * HEADS)
        mixed = jnp.dot(
            probabilities[of_request], values_ref[r], preferred_element_type=jnp.float32
        )
        mixed = mixed + own_prob[of_request] * new_values[r : r + 1, :]
        mixed = jnp.where(own_kv, mixed, 0.0)
        attended = mixed[:, :HEAD_DIM]
        for k in range(1, KV_HEADS):
            attended = attended + mixed[:, k * HEAD_DIM : (k + 1) * HEAD_DIM]
        for h in range(HEADS):
            stream_ref[r : r + 1, h * HEAD_DIM : (h + 1) * HEAD_DIM] = attended[h : h + 1, :]

    stream = residual_ref[...].astype(jnp.float32) + stream_ref[...]
    stream_ref[...] = stream
    average = jnp.mean(stream, axis=1, keepdims=True)
    centered = stream - average
    variance = jnp.mean(centered * centered, axis=1, keepdims=True)
    normed = (centered * lax.rsqrt(variance + NORM_EPS) * gain_ref[...]).astype(jnp.bfloat16)

    logits = lax.dot_general(
        normed, router_ref[...], (((1,), (1,)), ((), ())), preferred_element_type=jnp.float32
    )
    expert_iota = lax.broadcasted_iota(jnp.int32, (batch, EXPERTS), 1)
    ids = ids_ref[...]
    named = expert_iota == ids[:, 0:1]
    for j in range(1, TOPK):
        named = named | (expert_iota == ids[:, j : j + 1])
    top = jnp.max(jnp.where(named, logits, -jnp.inf), axis=1, keepdims=True)
    raised = jnp.where(named, jnp.exp(logits - top), 0.0)
    gates = raised / jnp.sum(raised, axis=1, keepdims=True)
    gates_high = gates.astype(jnp.bfloat16)
    gates_low = (gates - gates_high.astype(jnp.float32)).astype(jnp.bfloat16)

    mine = gathered.at[t, e, a]
    mine[:, :width] = normed
    mine[:, width:] = jnp.zeros((batch, 256), jnp.bfloat16)
    mine[:, width : width + EXPERTS] = gates_high
    mine[:, width + 128 : width + 128 + EXPERTS] = gates_low

    pl.semaphore_wait(barrier, partners)

    def attn_send(step):
        return pltpu.make_async_remote_copy(
            src_ref=gathered.at[t, e, a],
            dst_ref=gathered.at[t, e, a],
            send_sem=ga_send.at[step],
            recv_sem=ga_recv.at[step],
            device_id={"attn": lax.rem(a + step, n_attn)},
            device_id_type=MESH,
        )

    def attn_arrived(step):
        source = lax.rem(a + n_attn - step, n_attn)
        block = gathered.at[t, e, source]
        return pltpu.make_async_remote_copy(
            src_ref=block,
            dst_ref=block,
            send_sem=ga_send.at[step],
            recv_sem=ga_recv.at[step],
            device_id={"attn": source},
            device_id_type=MESH,
        )

    def expert_copy(step, back, reverse):
        source_a = lax.rem(a + n_attn - back, n_attn)
        source_e = lax.rem(e + n_expert - step, n_expert) if reverse else e
        target_e = lax.rem(e + n_expert - step, n_expert) if reverse else lax.rem(e + step, n_expert)
        block = gathered.at[t, source_e, source_a]
        return pltpu.make_async_remote_copy(
            src_ref=block,
            dst_ref=block,
            send_sem=gx_send.at[step, back],
            recv_sem=gx_recv.at[step, back],
            device_id={"expert": target_e},
            device_id_type=MESH,
        )

    def core_copy(cstep, step, back, reverse):
        source_a = lax.rem(a + n_attn - back, n_attn)
        source_e = lax.rem(e + n_expert - step, n_expert)
        other = lax.rem(t + n_tp - cstep, n_tp)
        source_t = other if reverse else t
        target = other if reverse else lax.rem(t + cstep, n_tp)
        block = gathered.at[source_t, source_e, source_a]
        return pltpu.make_async_remote_copy(
            src_ref=block,
            dst_ref=block,
            send_sem=gc_send.at[cstep, step, back],
            recv_sem=gc_recv.at[cstep, step, back],
            device_id={"tp": target},
            device_id_type=MESH,
        )

    for step in range(1, n_attn):
        attn_send(step).start()

    def forward_all(back, _):
        for step in range(1, n_expert):
            expert_copy(step, back, False).start()
        for cstep in range(1, n_tp):
            core_copy(cstep, 0, back, False).start()

    forward_all(0, None)
    start_weights(PACE[2])

    def arrived_then_forward(back, carry):
        attn_arrived(back).wait_recv()
        forward_all(back, None)
        return carry

    def crossed_then_forward(back, carry):
        for step in range(1, n_expert):
            expert_copy(step, back, True).wait_recv()
            for cstep in range(1, n_tp):
                core_copy(cstep, step, back, False).start()
        return carry

    def core_arrived(back, carry):
        for step in range(n_expert):
            for cstep in range(1, n_tp):
                core_copy(cstep, step, back, True).wait_recv()
        return carry

    for back in range(1, n_attn):
        arrived_then_forward(back, 0)
        start_weights(PACE[3])
    for back in range(n_attn):
        crossed_then_forward(back, 0)
        start_weights(PACE[4])
    start_weights(len(waiting))
    lax.fori_loop(0, n_attn, core_arrived, 0)

    per_stage = 16 // batch
    attn_stages = n_attn // per_stage

    def assemble(i, carry):
        at_t = i // (n_expert * attn_stages)
        at_e = lax.rem(i // attn_stages, n_expert)
        at_a = lax.rem(i, attn_stages) * per_stage
        for j in range(per_stage):
            stage[j * batch : (j + 1) * batch, :] = gathered[at_t, at_e, at_a + j].astype(
                jnp.float32
            )
        at = pl.ds(pl.multiple_of(i * 16, 16), 16)
        rows_ref[at, :] = stage[:, :width].astype(jnp.bfloat16)
        weights_ref[at, :] = stage[:, width : width + 128] + stage[:, width + 128 :]
        return carry

    lax.fori_loop(0, total_rows // 16, assemble, 0)

    block_rows = min(total_rows, 64)
    row_blocks = total_rows // block_rows
    lane = lax.broadcasted_iota(jnp.int32, (block_rows, 128), 1)

    by_last = (((1,), (1,)), ((), ()))

    def first_products(i, carry):
        for p in range(pieces):
            gate_copy(i, p).wait()
            up_copy(i, p).wait()

        def one_block(b, inner):
            at = pl.ds(pl.multiple_of(b * block_rows, block_rows), block_rows)
            gate_act = lax.dot_general(
                gate_ref[i], rows_ref[at, :], by_last, preferred_element_type=jnp.float32
            ).T
            up_act = lax.dot_general(
                up_ref[i], rows_ref[at, :], by_last, preferred_element_type=jnp.float32
            ).T
            valid = lane < EXPERTS
            chosen = jnp.where((lane == e * local + i) & valid, weights_ref[at, :], 0.0)
            scale = jnp.sum(chosen, axis=1, keepdims=True)
            hidden = gate_act / (1.0 + jnp.exp(-gate_act)) * up_act * scale
            hidden_ref[i, at, :] = hidden.astype(jnp.bfloat16)
            return inner

        lax.fori_loop(0, row_blocks, one_block, 0)
        return carry

    lax.fori_loop(0, local, first_products, 0)

    def core_sum(c, step, reverse):
        other = lax.rem(t + n_tp - step, n_tp) if reverse else lax.rem(t + step, n_tp)
        return pltpu.make_async_remote_copy(
            src_ref=part_b16.at[c, other],
            dst_ref=part_in.at[c, step],
            send_sem=rc_send.at[c, step],
            recv_sem=rc_recv.at[c, step],
            device_id={"tp": other},
            device_id_type=MESH,
        )

    def chip_sum(c, step, reverse):
        other = lax.rem(chip + chips - step, chips) if reverse else lax.rem(chip + step, chips)
        return pltpu.make_async_remote_copy(
            src_ref=quad_b16.at[c, other],
            dst_ref=quad_in.at[c, step],
            send_sem=ra_send.at[c, step],
            recv_sem=ra_recv.at[c, step],
            device_id={"expert": other // n_attn, "attn": lax.rem(other, n_attn)},
            device_id_type=MESH,
        )

    tp_rows = total_rows // n_tp
    tp_block = min(tp_rows, 32)

    def compute_chunk(c):
        for i in range(local):
            down_copy(c, i).wait()
        for at_t in range(n_tp):

            def one_block(b, inner, at_t=at_t):
                start = pl.multiple_of(b * tp_block, tp_block)
                at = pl.ds(start, tp_block)
                from_rows = pl.ds(pl.multiple_of(at_t * tp_rows + start, tp_block), tp_block)
                total = jnp.zeros((tp_block, chunk), jnp.float32)
                for i in range(local):
                    total = total + jnp.dot(
                        hidden_ref[i, from_rows, :],
                        down_ref[c, i],
                        preferred_element_type=jnp.float32,
                    )
                part_f32[c, at_t, at, :] = total
                part_b16[c, at_t, at, :] = total.astype(jnp.bfloat16)
                return inner

            lax.fori_loop(0, tp_rows // tp_block, one_block, 0)
        for step in range(1, n_tp):
            core_sum(c, step, False).start()

    def compute_chunk_whole(c):
        for i in range(local):
            down_copy(c, i).wait()
        total = jnp.dot(hidden_ref[0], down_ref[c, 0], preferred_element_type=jnp.float32)
        for i in range(1, local):
            total = total + jnp.dot(
                hidden_ref[i], down_ref[c, i], preferred_element_type=jnp.float32
            )
        for at_t in range(n_tp):
            rows = total[at_t * tp_rows : (at_t + 1) * tp_rows, :]
            part_f32[c, at_t] = rows
            part_b16[c, at_t] = rows.astype(jnp.bfloat16)
        for step in range(1, n_tp):
            core_sum(c, step, False).start()

    def send_chunk(c):
        for step in range(1, n_tp):
            core_sum(c, step, True).wait_recv()

        def one_block(b, carry):
            at = pl.ds(pl.multiple_of(b * 16, 16), 16)
            total = part_f32[c, t, at, :]
            for step in range(1, n_tp):
                total = total + part_in[c, step, at, :].astype(jnp.float32)
            for j in range(per_stage):
                rows = total[j * batch : (j + 1) * batch, :]
                quad_f32[c, b * per_stage + j] = rows
                quad_b16[c, b * per_stage + j] = rows.astype(jnp.bfloat16)
            return carry

        lax.fori_loop(0, tp_rows // 16, one_block, 0)

        def one_send(step, carry):
            chip_sum(c, step, False).start()
            return carry

        lax.fori_loop(1, chips, one_send, 0)

    def finish_chunk(c):
        columns = slice(c * chunk, (c + 1) * chunk)

        def one_arrival(step, total):
            chip_sum(c, step, True).wait_recv()
            return total + quad_in[c, step].astype(jnp.float32)

        total = lax.fori_loop(1, chips, one_arrival, stream_ref[:, columns] + quad_f32[c, chip])
        out_ref[:, columns] = total.astype(out_ref.dtype)

    compute = compute_chunk_whole if total_rows <= 64 else compute_chunk
    for c in range(chunks):
        compute(c)
        if c > 0:
            send_chunk(c - 1)
    send_chunk(chunks - 1)
    for c in range(chunks):
        finish_chunk(c)

    for step in range(1, n_attn):
        attn_send(step).wait_send()

    def sends_done(back, carry):
        for step in range(1, n_expert):
            expert_copy(step, back, False).wait_send()
        for step in range(n_expert):
            for cstep in range(1, n_tp):
                core_copy(cstep, step, back, False).wait_send()
        return carry

    lax.fori_loop(0, n_attn, sends_done, 0)
    for c in range(chunks):
        for step in range(1, n_tp):
            core_sum(c, step, False).wait_send()

        def one_left(step, carry, c=c):
            chip_sum(c, step, False).wait_send()
            return carry

        lax.fori_loop(1, chips, one_left, 0)


def body(
    residual,
    queries,
    new_keys,
    new_values,
    cache_keys,
    cache_values,
    lengths,
    norm_gain,
    router,
    expert_ids,
    w_gate,
    w_up,
    w_down,
):
    n_attn = lax.axis_size("attn")
    n_expert = lax.axis_size("expert")
    n_tp = lax.axis_size("tp")
    batch, width = residual.shape
    local, _, ff = w_gate.shape
    total_rows = n_attn * n_expert * n_tp * batch
    chunks = 2
    chunk = width // chunks
    tp_rows = total_rows // n_tp
    chips = n_expert * n_attn
    pieces = 2 if ff % 32 == 0 else 1
    vmem = pl.BlockSpec(memory_space=pltpu.VMEM)
    anywhere = pl.BlockSpec(memory_space=pl.ANY)
    dma = pltpu.SemaphoreType.DMA
    bf16, f32 = jnp.bfloat16, jnp.float32
    return pl.pallas_call(
        functools.partial(kernel, (n_attn, n_expert, n_tp, chunks)),
        out_shape=jax.ShapeDtypeStruct((batch, width), bf16),
        in_specs=[vmem] * 4
        + [pl.BlockSpec(memory_space=pltpu.SMEM)]
        + [vmem] * 3
        + [anywhere] * 5,
        out_specs=vmem,
        scratch_shapes=[
            pltpu.VMEM(cache_keys.shape, bf16),
            pltpu.VMEM(cache_values.shape, bf16),
            pltpu.VMEM((local, ff, width), bf16),
            pltpu.VMEM((local, ff, width), bf16),
            pltpu.VMEM((chunks, local, ff, chunk), bf16),
            pltpu.VMEM((batch, HEADS, HEAD_DIM), f32),
            pltpu.VMEM((batch, width), f32),
            pltpu.VMEM((n_tp, n_expert, n_attn, batch, width + 256), bf16),
            pltpu.VMEM((16, width + 256), f32),
            pltpu.VMEM((total_rows, width), bf16),
            pltpu.VMEM((total_rows, 128), f32),
            pltpu.VMEM((local, total_rows, ff), bf16),
            pltpu.VMEM((chunks, n_tp, tp_rows, chunk), f32),
            pltpu.VMEM((chunks, n_tp, tp_rows, chunk), bf16),
            pltpu.VMEM((chunks, n_tp, tp_rows, chunk), bf16),
            pltpu.VMEM((chunks, chips, batch, chunk), f32),
            pltpu.VMEM((chunks, chips, batch, chunk), bf16),
            pltpu.VMEM((chunks, chips, batch, chunk), bf16),
            dma((2,)),
            dma((local, pieces)),
            dma((local, pieces)),
            dma((chunks, local)),
            dma((n_attn,)),
            dma((n_attn,)),
            dma((n_expert, n_attn)),
            dma((n_expert, n_attn)),
            dma((n_tp, n_expert, n_attn)),
            dma((n_tp, n_expert, n_attn)),
            dma((chunks, n_tp)),
            dma((chunks, n_tp)),
            dma((chunks, chips)),
            dma((chunks, chips)),
        ],
        compiler_params=pltpu.CompilerParams(
            collective_id=0, has_side_effects=True, vmem_limit_bytes=63 * 1024 * 1024
        ),
    )(
        residual,
        queries,
        new_keys,
        new_values,
        lengths,
        norm_gain.reshape(1, width),
        router.T,
        expert_ids,
        cache_keys,
        cache_values,
        jnp.swapaxes(w_gate, 1, 2),
        jnp.swapaxes(w_up, 1, 2),
        w_down,
    )


def solution(mesh):
    rows = ("groups", "attn", "expert", "tp")
    return jax.shard_map(
        body,
        mesh=mesh,
        in_specs=(
            P(rows, None),
            P(rows, None),
            P(rows, None),
            P(rows, None),
            P(rows, None, None),
            P(rows, None, None),
            P(rows),
            P(),
            P(),
            P(rows, None),
            P("expert", None, ("attn", "tp")),
            P("expert", None, ("attn", "tp")),
            P("expert", ("attn", "tp"), None),
        ),
        out_specs=P(rows, None),
        check_vma=False,
    )
```
